32 devices in a mesh: groups: 2 (over x), view: 2 (over core), tile: 8 (over z, y).
Axes of the slice: x: 2, y: 2, z: 4, core: 2. Of those that a mesh axis runs over, the one named last changes fastest.
Arguments:
- features: bfloat16 [8, 64, 320, 128], P(('groups', 'view'), 'tile'), parts along dimension 0, may hold values from -6 to 6
- ref_views: int32 [8], P('groups'), parts along dimension 0, may hold values from 0 to 3, as said below
- intersection: int32 [8, 4], P('groups'), parts along dimension 0, may hold values from 0 to 1, as said below
- offsets: int32 [8, 4], P('groups'), parts along dimension 0, may hold values from 0 to 16, as said below
- conv_weight: bfloat16 [3, 3, 3, 32, 40], replicated, may hold values from -0.1875 to 0.1875
- conv_bias: float32 [32], replicated, may hold values from -1.5 to 1.5
Outputs:
- regularized: bfloat16 [8, 32, 32, 64, 128], P('groups', None, 'view', 'tile'), parts along dimension 0
The draws below stay inside these ranges and needn't reach their ends.
There are 2 independent parts, one for each index of `groups`. The reference program is written for one: setup_inputs(seed, part) draws one part's arguments, and reference() takes and returns one part's arrays. A program takes and returns all parts, laid end to end along the dimension named above; an argument that names none is the same for every part. Nothing has to cross between parts.
Inputs may be any that keep to these rules, and one draw needn't show every extreme that they name: `ref_views`: distinct views. `intersection`: never 1 at the reference's own view; every row has at least one source. `offsets`: the value 17 - 1 is taken at some source of some reference.
All inputs are finite; a program needn't handle non-finite values.
Results may differ from the reference program's by a relative error of at most 0.006.
Values may be sent and summed in bfloat16 or wider, within the bound.
A program may use at most 192 MiB of HBM per device.

```python
import jax
import jax.numpy as jnp
from jax import lax

C = 320
G = 40
OC = 32
ND = 32
OFF = 17
W = 128
V_DEV = 2
NREF = 4
VIEWS = 4
NROWS = 64
N_VIEW = 2


def survey_layout(key):
    ordering = jax.random.permutation(jax.random.fold_in(key, 11), VIEWS)
    chosen_views = ordering[:NREF]
    nudges = jax.random.randint(jax.random.fold_in(key, 12), (NREF,), 1, VIEWS)
    partner = ordering[(jnp.arange(NREF) + nudges) % VIEWS]
    columns = jnp.arange(VIEWS)
    forced = columns[None, :] == partner[:, None]
    itself = columns[None, :] == chosen_views[:, None]
    tosses = jax.random.randint(jax.random.fold_in(key, 13), (NREF, VIEWS), 0, 2)
    intersection = jnp.where(itself, 0, jnp.where(forced, 1, tosses)).astype(jnp.int32)
    starts = jax.random.randint(jax.random.fold_in(key, 14), (NREF, VIEWS), 0, OFF)
    lucky = jax.random.randint(jax.random.fold_in(key, 15), (), 0, NREF)
    peaked = forced & (jnp.arange(NREF)[:, None] == lucky)
    starts = jnp.where(peaked, OFF - 1, starts).astype(jnp.int32)
    return (chosen_views.astype(jnp.int32), intersection, starts)


def draw_ref_views(key, part):
    return survey_layout(key)[0]


def draw_intersection(key, part):
    return survey_layout(key)[1]


def draw_offsets(key, part):
    return survey_layout(key)[2]


def level_of(stream_key, shape, cuts, low, top_value):
    factor_of, own = 1.0, jax.random.fold_in(stream_key, 6)
    for axis_at, parts in cuts:
        heights = jnp.exp(jax.random.uniform(jax.random.fold_in(own, axis_at), (parts,), jnp.float32, low / len(cuts), top_value / len(cuts)))
        factor_of = factor_of * jnp.repeat(heights, shape[axis_at] // parts).reshape([-1 if axis == axis_at else 1 for axis in range(len(shape))])
    return factor_of


def bell_draw(rng, extent, width, limit, cuts=(), dtype=jnp.bfloat16):
    array = width * jax.random.normal(rng, extent, jnp.float32)
    if cuts:
        array = array * level_of(rng, extent, cuts, -0.22, 0.18)
    return jnp.clip(array, -limit, limit).astype(dtype)


def setup_inputs(seed: int = 0, part: int = 0) -> dict:
    seeds = jax.random.split(jax.random.key(seed), 7)
    own_keys = jax.random.split(jax.random.fold_in(seeds[6], part), 7)
    features = bell_draw(own_keys[0], (VIEWS, NROWS, C, W), 1.0, 6.0, ((0, 2), (1, 8)))
    ref_views = draw_ref_views(jax.random.fold_in(jax.random.fold_in(seeds[6], part), 71), part)
    intersection = draw_intersection(jax.random.fold_in(jax.random.fold_in(seeds[6], part), 71), part)
    offsets = draw_offsets(jax.random.fold_in(jax.random.fold_in(seeds[6], part), 71), part)
    conv_weight = bell_draw(seeds[4], (3, 3, 3, OC, G), (27 * G) ** -0.5, 0.1875)
    conv_bias = bell_draw(seeds[5], (OC,), 0.3, 1.5, (), jnp.float32)
    return {"features": features, "ref_views": ref_views, "intersection": intersection, "offsets": offsets, "conv_weight": conv_weight, "conv_bias": conv_bias}


def group_products(reference_rows, source_rows, groups):
    rows, channels, columns = reference_rows.shape
    left = reference_rows.reshape(rows, groups, channels // groups, columns).astype(jnp.float32)
    right = source_rows.reshape(rows, groups, channels // groups, columns).astype(jnp.float32)
    summed = jnp.einsum("rgcw,rgcw->grw", left, right)
    return summed * (1.0 / (channels // groups))


def correlate(reference_rows, window, groups, depth):
    rows = reference_rows.shape[0]
    layers = [group_products(reference_rows, window[depth - 1 - disparity: depth - 1 - disparity + rows], groups) for disparity in range(depth)]
    return jnp.stack(layers, axis=1)


def convolve(volume, conv_weight, conv_bias):
    groups, depth, rows, columns = volume.shape
    padded = jnp.pad(volume, ((0, 0), (1, 1), (1, 1), (1, 1))).astype(jnp.float32)
    weight = conv_weight.astype(jnp.float32)
    total = jnp.zeros((conv_weight.shape[3], depth, rows, columns), jnp.float32)
    for depth_tap in range(3):
        for row_tap in range(3):
            for column_tap in range(3):
                piece = padded[:, depth_tap:depth_tap + depth, row_tap:row_tap + rows, column_tap:column_tap + columns]
                total = total + jnp.einsum("og,gdrw->odrw", weight[depth_tap, row_tap, column_tap], piece)
    return jax.nn.relu(total + conv_bias[:, None, None, None]).astype(jnp.bfloat16)


def reference(features, ref_views, intersection, offsets, conv_weight, conv_bias):
    views, rows, channels, columns = features.shape
    reach = ND + OFF - 1
    padded = jnp.pad(features, ((0, 0), (reach, 0), (0, 0), (0, 0)))
    results = []
    for slot in range(NREF):
        chosen = lax.dynamic_index_in_dim(features, ref_views[slot].astype(jnp.int32), 0, keepdims=False)
        blocks = []
        for owner in range(N_VIEW):
            partial_value = jnp.zeros((G, ND, rows, columns), jnp.float32)
            for inner in range(V_DEV):
                view = owner * V_DEV + inner
                start = (reach - offsets[slot, view] - (ND - 1)).astype(jnp.int32)
                window = lax.dynamic_slice_in_dim(padded[view], start, rows + ND - 1, 0)
                partial_value = partial_value + intersection[slot, view].astype(jnp.float32) * correlate(chosen, window, G, ND)
            blocks.append(lax.optimization_barrier(partial_value.astype(jnp.bfloat16)).astype(jnp.float32))
        total = blocks[0]
        for extra in blocks[1:]:
            total = total + extra
        scale = 1.0 / jnp.sum(intersection[slot]).astype(jnp.float32)
        cost = (total * scale).astype(jnp.bfloat16)
        results.append(convolve(cost, conv_weight, conv_bias))
    return jnp.stack(results, axis=0)
```

```python
import functools

import jax
import jax.numpy as jnp
from jax import lax
from jax.experimental import pallas as pl
from jax.experimental.pallas import tpu as pltpu
from jax.sharding import PartitionSpec as P

ND = 32
OFF = 17
BELOW = 6
MESH = pl.DeviceIdType.MESH
PARTS = 2


def gather_kernel(count, feat, ext, zeros, local_sem, zero_sem, z_send, z_recv, pair_send, pair_recv, core_send, core_recv, edge_send, edge_recv):
    views, rows = feat.shape[0], feat.shape[1]
    tile = lax.axis_index("tile")
    core = lax.axis_index("view")
    other = 1 - core
    odd = tile % 2
    partner = tile + 1 - 2 * odd
    top = BELOW * rows
    step = rows // PARTS
    pieces = [(v, h * step) for v in range(views) for h in range(PARTS)]

    barrier = pltpu.get_barrier_semaphore()
    pl.semaphore_signal(barrier, inc=1, device_id={"view": other}, device_id_type=MESH)
    peers = jnp.int32(1)
    for shift, both in ((2, False), (-2, False), (1, True), (-1, True)):
        there = (tile + shift >= 0) & (tile + shift < count)
        peers = peers + jnp.where(there, 2 if both else 1, 0)

        @pl.when(there)
        def _(shift=shift, both=both):
            pl.semaphore_signal(barrier, inc=1, device_id={"tile": tile + shift}, device_id_type=MESH)
            if both:
                pl.semaphore_signal(barrier, inc=1, device_id={"tile": tile + shift, "view": other}, device_id_type=MESH)

    pl.semaphore_wait(barrier, peers)

    def slot(q, piece):
        v, row = piece
        return ext.at[core * views + v, pl.ds((BELOW - q) * rows + row, step)]

    def mine(piece):
        v, row = piece
        return feat.at[v, pl.ds(row, step)]

    def z_copy(p, n):
        src = mine(pieces[n]) if p == 0 else slot(2 * p, pieces[n])
        return pltpu.make_async_remote_copy(src, slot(2 * p + 2, pieces[n]), z_send.at[p, n], z_recv.at[p, n], device_id={"tile": tile + 2}, device_id_type=MESH)

    def even_copy(k, n):
        src = mine(pieces[n]) if k == 0 else slot(2 * k, pieces[n])
        return pltpu.make_async_remote_copy(src, slot(2 * k + 1, pieces[n]), pair_send.at[k, n], pair_recv.at[k, n], device_id={"tile": partner}, device_id_type=MESH)

    def odd_copy(k, n):
        return pltpu.make_async_remote_copy(slot(2 * k + 2, pieces[n]), slot(2 * k + 1, pieces[n]), pair_send.at[k, n], pair_recv.at[k, n], device_id={"tile": partner}, device_id_type=MESH)

    def core_copy(q, n):
        src = mine(pieces[n]) if q == 0 else slot(q, pieces[n])
        return pltpu.make_async_remote_copy(src, slot(q, pieces[n]), core_send.at[q, n], core_recv.at[q, n], device_id={"view": other}, device_id_type=MESH)

    def edge_copy(n):
        return pltpu.make_async_remote_copy(
            feat.at[:, pl.ds(0, 1)],
            ext.at[pl.ds(core * views, views), pl.ds(top + rows, 1)],
            edge_send.at[n],
            edge_recv.at[n],
            device_id={"tile": tile - 1} if n == 0 else {"tile": tile - 1, "view": other},
            device_id_type=MESH,
        )

    def local_copy():
        return pltpu.make_async_copy(feat, ext.at[pl.ds(core * views, views), pl.ds(top, rows)], local_sem)

    def zero_copy(q, v):
        return pltpu.make_async_copy(zeros, ext.at[v, pl.ds((BELOW - q) * rows, rows)], zero_sem.at[q, v])

    def zero_edge(v):
        return pltpu.make_async_copy(zeros.at[pl.ds(0, 1)], ext.at[v, pl.ds(top + rows, 1)], zero_sem.at[0, v])

    last = tile == count - 1
    upward = tile + 2 < count
    everything = range(len(pieces))

    @pl.when(upward)
    def _():
        for n in everything:
            z_copy(0, n).start()

    @pl.when(odd == 0)
    def _():
        for n in everything:
            even_copy(0, n).start()

    @pl.when(tile >= 1)
    def _():
        for n in range(2):
            edge_copy(n).start()

    for n in everything:
        core_copy(0, n).start()
    local_copy().start()

    @pl.when((tile < BELOW) | last)
    def _():
        zeros[...] = jnp.zeros_like(zeros)

    for q in range(1, BELOW + 1):

        @pl.when(tile < q)
        def _(q=q):
            for v in range(2 * views):
                zero_copy(q, v).start()

    @pl.when(last)
    def _():
        for v in range(2 * views):
            zero_edge(v).start()

    for p in range(3):
        for n in everything:

            @pl.when(tile >= 2 * p + 2)
            def _(p=p, n=n):
                z_copy(p, n).wait_recv()
                if p < 2:

                    @pl.when(upward)
                    def _():
                        z_copy(p + 1, n).start()

                    @pl.when(odd == 0)
                    def _():
                        even_copy(p + 1, n).start()

                @pl.when(odd == 1)
                def _():
                    odd_copy(p, n).start()

                core_copy(2 * p + 2, n).start()

            @pl.when(tile >= 2 * p + 1)
            def _(p=p, n=n):
                even_copy(p, n).wait_recv()
                core_copy(2 * p + 1, n).start()

    for n in everything:
        for p in range(3):

            @pl.when(upward & (tile >= 2 * p))
            def _(p=p, n=n):
                z_copy(p, n).wait_send()

            @pl.when((odd == 0) & (tile >= 2 * p))
            def _(p=p, n=n):
                even_copy(p, n).wait_send()

            @pl.when((odd == 1) & (tile >= 2 * p + 2))
            def _(p=p, n=n):
                odd_copy(p, n).wait_send()

        for q in range(BELOW + 1):

            @pl.when(tile >= q)
            def _(q=q, n=n):
                core_copy(q, n).wait()

    @pl.when(tile >= 1)
    def _():
        for n in range(2):
            edge_copy(n).wait_send()

    @pl.when(jnp.logical_not(last))
    def _():
        for n in range(2):
            pltpu.make_async_remote_copy(
                feat.at[:, pl.ds(0, 1)],
                ext.at[pl.ds((core if n == 0 else other) * views, views), pl.ds(top + rows, 1)],
                edge_send.at[n],
                edge_recv.at[n],
                device_id={"view": other},
                device_id_type=MESH,
            ).wait_recv()

    local_copy().wait()
    for q in range(1, BELOW + 1):

        @pl.when(tile < q)
        def _(q=q):
            for v in range(2 * views):
                zero_copy(q, v).wait()

    @pl.when(last)
    def _():
        for v in range(2 * views):
            zero_edge(v).wait()


def gathered(features, count):
    views, rows, channels, columns = features.shape
    n = views * PARTS
    dma = pltpu.SemaphoreType.DMA
    return pl.pallas_call(
        functools.partial(gather_kernel, count),
        out_shape=jax.ShapeDtypeStruct((2 * views, (BELOW + 1) * rows + 1, channels, columns), features.dtype),
        in_specs=[pl.BlockSpec(memory_space=pl.ANY)],
        out_specs=pl.BlockSpec(memory_space=pl.ANY),
        scratch_shapes=[
            pltpu.VMEM((rows, channels, columns), features.dtype),
            dma,
            dma((BELOW + 1, 2 * views)),
            dma((3, n)),
            dma((3, n)),
            dma((3, n)),
            dma((3, n)),
            dma((BELOW + 1, n)),
            dma((BELOW + 1, n)),
            dma((2,)),
            dma((2,)),
        ],
        compiler_params=pltpu.CompilerParams(collective_id=0, has_side_effects=True),
    )(features)


def volume_kernel(chunks, refs, marks, offs, ext, select, weight, bias, out, moved, cost, taps, ring):
    chunk = pl.program_id(0)
    half = lax.axis_index("view")
    slots = refs.shape[0]
    views, span, width, columns = ext.shape
    planes = ND // 2 + 1
    tall = 10
    own = span - tall
    sums = planes + tall - 1
    groups = width // 8
    first = own - (planes - 1) - 15 * half

    def correlate(slot, _):
        sources = [(marks[slot, v].astype(jnp.float32).astype(jnp.bfloat16), first - offs[slot, v]) for v in range(views)]
        for m in range(sums):
            rows = [ext[v, start + m] * mark for v, (mark, start) in enumerate(sources)]
            moved[pl.ds(m * width, width)] = (rows[0] + rows[1]) + (rows[2] + rows[3])
        view = refs[slot]
        for low, many in ((0, 4), (4, 4), (8, 2)):
            anchor = ext[view, pl.ds(own + low, many)].reshape(many * width, columns)
            mat = select[: many * groups, : many * width]
            for k in range(0, planes, 2):
                ks = [k, k + 1] if k + 1 < planes else [k]
                parts = [moved[pl.ds((low - kk + planes - 1) * width, many * width)] * anchor for kk in ks]
                block = jnp.concatenate(parts, axis=1) if len(parts) > 1 else parts[0]
                got = jnp.dot(mat, block, preferred_element_type=jnp.float32)
                for n, kk in enumerate(ks):
                    for row in range(many):
                        cost[slot, kk, low + row, chunk] = got[row * groups : (row + 1) * groups, n * columns : (n + 1) * columns]
        return 0

    lax.fori_loop(0, slots, correlate, 0)

    @pl.when(chunk == chunks - 1)
    def _():
        lane = lax.broadcasted_iota(jnp.int32, (chunks * groups, columns), 1)

        def regularize(slot, _):
            total = marks[slot, 0]
            for v in range(1, views):
                total = total + marks[slot, v]
            scale = 0.125 / jnp.full((chunks * groups, columns), total.astype(jnp.float32))
            taps[(planes) * half] = jnp.zeros_like(taps[0])
            spare = jnp.zeros((128 - 3 * chunks * groups, columns), jnp.float32)

            def spread(k, _):
                for row in range(tall):
                    here = cost[slot, k, row].reshape(chunks * groups, columns) * scale
                    left = jnp.where(lane == 0, 0.0, pltpu.roll(here, 1, 1))
                    right = jnp.where(lane == columns - 1, 0.0, pltpu.roll(here, columns - 1, 1))
                    block = jnp.concatenate([left, here, right, spare], axis=0)
                    taps[k + 1 - half, pl.ds(row * 128, 128)] = block.astype(jnp.bfloat16)
                return 0

            lax.fori_loop(0, planes, spread, 0)

            def convolve(plane, _):
                for row in range(0, 8, 2):
                    block = jnp.concatenate([taps[plane, pl.ds((row + n) * 128, 384)] for n in range(2)], axis=1)
                    got = jnp.dot(weight[...], block, preferred_element_type=jnp.float32)
                    for n in range(2):
                        piece = got[:, n * columns : (n + 1) * columns]
                        ring[2, row + n] = ring[1, row + n] + piece[64:]
                        ring[1, row + n] = ring[0, row + n] + piece[32:64]
                        ring[0, row + n] = piece[:32]

                @pl.when(plane >= 2)
                def _():
                    done = jnp.maximum(ring[2] + bias[...][None], 0.0)
                    out[slot, :, plane - 2] = jnp.swapaxes(done, 0, 1).astype(jnp.bfloat16)

                return 0

            lax.fori_loop(0, planes + 1, convolve, 0)
            return 0

        lax.fori_loop(0, slots, regularize, 0)


def volume(ext, refs, marks, offs, conv_weight, conv_bias):
    views, span, channels, columns = ext.shape
    slots = refs.shape[0]
    made, groups = conv_weight.shape[3], conv_weight.shape[4]
    width = 64
    chunks = channels // width
    small = width // 8
    planes = ND // 2 + 1
    weight = jnp.transpose(conv_weight, (0, 3, 1, 2, 4)).reshape(3 * made, 3, 3 * groups)
    weight = jnp.pad(weight, ((0, 0), (0, 0), (0, 128 - 3 * groups))).reshape(3 * made, 384)
    select = (jnp.arange(4 * small)[:, None] == jnp.arange(4 * width)[None, :] // 8).astype(jnp.bfloat16)
    bias = jnp.broadcast_to(conv_bias[:, None], (made, columns))
    smem = pl.BlockSpec(memory_space=pltpu.SMEM)
    shape = (slots, made, ND // 2, 8, columns)
    return pl.pallas_call(
        functools.partial(volume_kernel, chunks),
        grid=(chunks,),
        out_shape=jax.ShapeDtypeStruct(shape, jnp.bfloat16),
        in_specs=[
            smem,
            smem,
            smem,
            pl.BlockSpec((views, span, width, columns), lambda c: (0, 0, c, 0)),
            pl.BlockSpec(select.shape, lambda c: (0, 0)),
            pl.BlockSpec(weight.shape, lambda c: (0, 0)),
            pl.BlockSpec(bias.shape, lambda c: (0, 0)),
        ],
        out_specs=pl.BlockSpec(shape, lambda c: (0, 0, 0, 0, 0)),
        scratch_shapes=[
            pltpu.VMEM(((planes + 9) * width, columns), jnp.bfloat16),
            pltpu.VMEM((slots, planes, 10, chunks, small, columns), jnp.float32),
            pltpu.VMEM((planes + 1, 10 * 128, columns), jnp.bfloat16),
            pltpu.VMEM((3, 8, made, columns), jnp.float32),
        ],
        compiler_params=pltpu.CompilerParams(vmem_limit_bytes=56 * 1024 * 1024),
    )(refs, marks, offs, ext, select, weight, bias)


def shards(count, features, ref_views, intersection, offsets, conv_weight, conv_bias):
    ext = gathered(features, count)
    return volume(ext, ref_views, intersection, offsets, conv_weight, conv_bias)


def solution(mesh):
    placed = (
        P(("groups", "view"), "tile", None, None),
        P("groups"),
        P("groups", None),
        P("groups", None),
        P(),
        P(),
    )
    return jax.shard_map(
        functools.partial(shards, mesh.shape["tile"]),
        mesh=mesh,
        in_specs=placed,
        out_specs=P("groups", None, "view", "tile", None),
        check_vma=False,
    )
```

```python
import functools

import jax
import jax.numpy as jnp
from jax import lax
from jax.experimental import pallas as pl
from jax.experimental.pallas import tpu as pltpu
from jax.sharding import PartitionSpec as P

ND = 32
OFF = 17
BELOW = 6
MESH = pl.DeviceIdType.MESH
WIDTH = 64


def gather_kernel(count, feat, refs, marks, offs, select, out, *scratch):
    views, rows, channels, columns = feat.shape
    parts = channels // WIDTH
    ext, rest = scratch[:parts], scratch[parts:]
    moved, cost, local_sem, out_sem, z_send, z_recv, pair_send, pair_recv, core_send, core_recv, edge_send, edge_recv = rest
    tile = lax.axis_index("tile")
    core = lax.axis_index("view")
    other = 1 - core
    odd = tile % 2
    partner = tile + 1 - 2 * odd
    top = BELOW * rows

    barrier = pltpu.get_barrier_semaphore()
    pl.semaphore_signal(barrier, inc=1, device_id={"view": other}, device_id_type=MESH)
    peers = jnp.int32(1)
    for shift, both in ((2, False), (-2, False), (1, True), (-1, True)):
        there = (tile + shift >= 0) & (tile + shift < count)
        peers = peers + jnp.where(there, 2 if both else 1, 0)

        @pl.when(there)
        def _(shift=shift, both=both):
            pl.semaphore_signal(barrier, inc=1, device_id={"tile": tile + shift}, device_id_type=MESH)
            if both:
                pl.semaphore_signal(barrier, inc=1, device_id={"tile": tile + shift, "view": other}, device_id_type=MESH)

    pl.semaphore_wait(barrier, peers)

    def slot(q, n):
        return ext[n].at[pl.ds(core * views, views), pl.ds((BELOW - q) * rows, rows)]

    def mine(n):
        return feat.at[:, :, pl.ds(n * WIDTH, WIDTH)]

    def z_copy(p, n):
        src = mine(n) if p == 0 else slot(2 * p, n)
        return pltpu.make_async_remote_copy(src, slot(2 * p + 2, n), z_send.at[p, n], z_recv.at[p, n], device_id={"tile": tile + 2}, device_id_type=MESH)

    def even_copy(k, n):
        src = mine(n) if k == 0 else slot(2 * k, n)
        return pltpu.make_async_remote_copy(src, slot(2 * k + 1, n), pair_send.at[k, n], pair_recv.at[k, n], device_id={"tile": partner}, device_id_type=MESH)

    def odd_copy(k, n):
        return pltpu.make_async_remote_copy(slot(2 * k + 2, n), slot(2 * k + 1, n), pair_send.at[k, n], pair_recv.at[k, n], device_id={"tile": partner}, device_id_type=MESH)

    def core_copy(q, n):
        src = mine(n) if q == 0 else slot(q, n)
        return pltpu.make_async_remote_copy(src, slot(q, n), core_send.at[q, n], core_recv.at[q, n], device_id={"view": other}, device_id_type=MESH)

    def edge_copy(n, far, side):
        return pltpu.make_async_remote_copy(
            feat.at[:, pl.ds(0, 1), pl.ds(n * WIDTH, WIDTH)],
            ext[n].at[pl.ds(side * views, views), pl.ds(top + rows, 1)],
            edge_send.at[far, n],
            edge_recv.at[far, n],
            device_id={"tile": tile - 1, "view": other if far else core},
            device_id_type=MESH,
        )

    def local_copy(n):
        return pltpu.make_async_copy(mine(n), slot(0, n), local_sem.at[n])

    def out_copy(n):
        return pltpu.make_async_copy(cost.at[n], out.at[n], out_sem.at[n])

    def blank(low, many):
        for n in everything:
            for v in range(2 * views):
                ext[n][v, low : low + many] = jnp.zeros((many, WIDTH, columns), feat.dtype)

    last = tile == count - 1
    upward = tile + 2 < count
    everything = range(parts)

    @pl.when(upward)
    def _():
        for n in everything:
            z_copy(0, n).start()

    @pl.when(odd == 0)
    def _():
        for n in everything:
            even_copy(0, n).start()

    for n in everything:
        local_copy(n).start()
        core_copy(0, n).start()

    @pl.when(tile >= 1)
    def _():
        for n in everything:
            for far in range(2):
                edge_copy(n, far, core).start()

    for q in range(1, BELOW + 1):

        @pl.when(tile < q)
        def _(q=q):
            blank((BELOW - q) * rows, rows)

    @pl.when(last)
    def _():
        blank(top + rows, 1)

    def compute(n):
        for q in range(BELOW + 1):

            @pl.when(tile >= q)
            def _(q=q):
                core_copy(q, n).wait_recv()

        @pl.when(jnp.logical_not(last))
        def _():
            for far in range(2):
                edge_copy(n, far, other if far else core).wait_recv()

        local_copy(n).wait()
        correlate(ext[n], refs, marks, offs, select, moved, cost.at[n], core)
        out_copy(n).start()

    for p in range(3):
        for n in everything:

            @pl.when(tile >= 2 * p + 2)
            def _(p=p, n=n):
                z_copy(p, n).wait_recv()
                if p < 2:

                    @pl.when(upward)
                    def _():
                        z_copy(p + 1, n).start()

                    @pl.when(odd == 0)
                    def _():
                        even_copy(p + 1, n).start()

                @pl.when(odd == 1)
                def _():
                    odd_copy(p, n).start()

                core_copy(2 * p + 2, n).start()

            @pl.when(tile >= 2 * p + 1)
            def _(p=p, n=n):
                even_copy(p, n).wait_recv()
                core_copy(2 * p + 1, n).start()

            if p == 2 and n > 0:
                compute(n - 1)

    compute(parts - 1)

    for n in everything:
        for p in range(3):

            @pl.when(upward & (tile >= 2 * p))
            def _(p=p, n=n):
                z_copy(p, n).wait_send()

            @pl.when((odd == 0) & (tile >= 2 * p))
            def _(p=p, n=n):
                even_copy(p, n).wait_send()

            @pl.when((odd == 1) & (tile >= 2 * p + 2))
            def _(p=p, n=n):
                odd_copy(p, n).wait_send()

        for q in range(BELOW + 1):

            @pl.when(tile >= q)
            def _(q=q, n=n):
                core_copy(q, n).wait_send()

        @pl.when(tile >= 1)
        def _(n=n):
            for far in range(2):
                edge_copy(n, far, core).wait_send()

        out_copy(n).wait()


def correlate(ext, refs, marks, offs, select, moved, cost, half):
    slots = refs.shape[0]
    views, span, width, columns = ext.shape
    planes = ND // 2 + 1
    tall = 10
    own = span - tall
    sums = planes + tall - 1
    first = own - (planes - 1) - 15 * half

    def one(slot, _):
        sources = [(marks[slot, v].astype(jnp.float32).astype(jnp.bfloat16), first - offs[slot, v]) for v in range(views)]
        total = marks[slot, 0]
        for v in range(1, views):
            total = total + marks[slot, v]
        scale = 0.125 / jnp.full((8, columns), total.astype(jnp.float32))
        for m in range(sums):
            rows = [ext[v, start + m] * mark for v, (mark, start) in enumerate(sources)]
            moved[m * width : (m + 1) * width] = (rows[0] + rows[1]) + (rows[2] + rows[3])
        view = refs[slot]
        for low, many in ((0, 4), (4, 4), (8, 2)):
            anchor = ext[view, own + low : own + low + many].reshape(many * width, columns)
            mat = select[: many * 8, : many * width]
            factor = jnp.concatenate([scale] * many, axis=0)
            for k in range(0, planes, 2):
                ks = [k, k + 1] if k + 1 < planes else [k]
                blocks = []
                for kk in ks:
                    at = (low - kk + planes - 1) * width
                    blocks.append(moved[at : at + many * width] * anchor)
                block = jnp.concatenate(blocks, axis=1) if len(blocks) > 1 else blocks[0]
                got = jnp.dot(mat, block, preferred_element_type=jnp.float32)
                for n, kk in enumerate(ks):
                    cost[slot, kk, low * 8 : (low + many) * 8] = (got[:, n * columns : (n + 1) * columns] * factor).astype(jnp.bfloat16)
        return 0

    lax.fori_loop(0, slots, one, 0)


def gathered(features, refs, marks, offs, count):
    views, rows, channels, columns = features.shape
    slots = refs.shape[0]
    n = channels // WIDTH
    planes = ND // 2 + 1
    span = (BELOW + 1) * rows + 1
    select = (jnp.arange(32)[:, None] == jnp.arange(4 * WIDTH)[None, :] // 8).astype(jnp.bfloat16)
    dma = pltpu.SemaphoreType.DMA
    shape = (n, slots, planes, 80, columns)
    smem = pl.BlockSpec(memory_space=pltpu.SMEM)
    return pl.pallas_call(
        functools.partial(gather_kernel, count),
        out_shape=jax.ShapeDtypeStruct(shape, features.dtype),
        in_specs=[pl.BlockSpec(memory_space=pl.ANY), smem, smem, smem, pl.BlockSpec(memory_space=pltpu.VMEM)],
        out_specs=pl.BlockSpec(memory_space=pl.ANY),
        scratch_shapes=[pltpu.VMEM((2 * views, span, WIDTH, columns), features.dtype) for _ in range(n)]
        + [
            pltpu.VMEM(((planes + 9) * WIDTH, columns), features.dtype),
            pltpu.VMEM(shape, features.dtype),
            dma((n,)),
            dma((n,)),
            dma((3, n)),
            dma((3, n)),
            dma((3, n)),
            dma((3, n)),
            dma((BELOW + 1, n)),
            dma((BELOW + 1, n)),
            dma((2, n)),
            dma((2, n)),
        ],
        compiler_params=pltpu.CompilerParams(collective_id=0, has_side_effects=True, vmem_limit_bytes=48 * 1024 * 1024),
    )(features, refs, marks, offs, select)


def volume_kernel(cost, weight, bias, out, taps, ring):
    half = lax.axis_index("view")
    parts, planes, columns = cost.shape[0], cost.shape[2], cost.shape[4]
    tall = 10
    groups = parts * 8
    lane = lax.broadcasted_iota(jnp.int32, (groups, columns), 1)
    spare = jnp.zeros((128 - 3 * groups, columns), jnp.float32)
    taps[planes * half] = jnp.zeros_like(taps[0])

    def spread(k, _):
        for pair in range(0, tall, 2):
            both = [cost[n, 0, k, pair * 8 : pair * 8 + 16].astype(jnp.float32) for n in range(parts)]
            for row in range(2):
                here = jnp.concatenate([one[row * 8 : row * 8 + 8] for one in both], axis=0)
                left = jnp.where(lane == 0, 0.0, pltpu.roll(here, 1, 1))
                right = jnp.where(lane == columns - 1, 0.0, pltpu.roll(here, columns - 1, 1))
                block = jnp.concatenate([left, here, right, spare], axis=0)
                taps[k + 1 - half, (pair + row) * 128 : (pair + row + 1) * 128] = block.astype(jnp.bfloat16)
        return 0

    lax.fori_loop(0, planes, spread, 0)

    def convolve(plane, _):
        for row in range(0, 8, 2):
            block = jnp.concatenate([taps[plane, (row + n) * 128 : (row + n + 3) * 128] for n in range(2)], axis=1)
            got = jnp.dot(weight[...], block, preferred_element_type=jnp.float32)
            for n in range(2):
                piece = got[:, n * columns : (n + 1) * columns]
                ring[2, row + n] = ring[1, row + n] + piece[64:]
                ring[1, row + n] = ring[0, row + n] + piece[32:64]
                ring[0, row + n] = piece[:32]

        @pl.when(plane >= 2)
        def _():
            done = jnp.maximum(ring[2] + bias[...][None], 0.0)
            out[0, :, plane - 2] = jnp.swapaxes(done, 0, 1).astype(jnp.bfloat16)

        return 0

    lax.fori_loop(0, planes + 1, convolve, 0)


def volume(cost, conv_weight, conv_bias):
    parts, slots, planes, tall, columns = cost.shape
    made, groups = conv_weight.shape[3], conv_weight.shape[4]
    weight = jnp.transpose(conv_weight, (0, 3, 1, 2, 4)).reshape(3 * made, 3, 3 * groups)
    weight = jnp.pad(weight, ((0, 0), (0, 0), (0, 128 - 3 * groups))).reshape(3 * made, 384)
    bias = jnp.broadcast_to(conv_bias[:, None], (made, columns))
    shape = (slots, made, ND // 2, 8, columns)
    return pl.pallas_call(
        volume_kernel,
        grid=(slots,),
        out_shape=jax.ShapeDtypeStruct(shape, jnp.bfloat16),
        in_specs=[
            pl.BlockSpec((parts, 1, planes, tall, columns), lambda r: (0, r, 0, 0, 0)),
            pl.BlockSpec(weight.shape, lambda r: (0, 0)),
            pl.BlockSpec(bias.shape, lambda r: (0, 0)),
        ],
        out_specs=pl.BlockSpec((1,) + shape[1:], lambda r: (r, 0, 0, 0, 0)),
        scratch_shapes=[
            pltpu.VMEM((planes + 1, 10 * 128, columns), jnp.bfloat16),
            pltpu.VMEM((3, 8, made, columns), jnp.float32),
        ],
        compiler_params=pltpu.CompilerParams(vmem_limit_bytes=32 * 1024 * 1024),
    )(cost, weight, bias)


def shards(count, features, ref_views, intersection, offsets, conv_weight, conv_bias):
    cost = gathered(features, ref_views, intersection, offsets, count)
    return volume(cost, conv_weight, conv_bias)


def solution(mesh):
    placed = (
        P(("groups", "view"), "tile", None, None),
        P("groups"),
        P("groups", None),
        P("groups", None),
        P(),
        P(),
    )
    return jax.shard_map(
        functools.partial(shards, mesh.shape["tile"]),
        mesh=mesh,
        in_specs=placed,
        out_specs=P("groups", None, "view", "tile", None),
        check_vma=False,
    )
```

```python
import functools

import jax
import jax.numpy as jnp
from jax import lax
from jax.experimental import pallas as pl
from jax.experimental.pallas import tpu as pltpu
from jax.sharding import PartitionSpec as P

ND = 32
OFF = 17
BELOW = 6
MESH = pl.DeviceIdType.MESH
WIDTH = 64


def gather_kernel(count, feat, refs, marks, offs, select, out, *scratch):
    views, rows, channels, columns = feat.shape
    parts = channels // WIDTH
    ext, rest = scratch[:parts], scratch[parts:]
    moved, cost, local_sem, out_sem, z_send, z_recv, pair_send, pair_recv, core_send, core_recv, edge_send, edge_recv = rest
    tile = lax.axis_index("tile")
    core = lax.axis_index("view")
    other = 1 - core
    odd = tile % 2
    partner = tile + 1 - 2 * odd
    top = BELOW * rows

    barrier = pltpu.get_barrier_semaphore()
    pl.semaphore_signal(barrier, inc=1, device_id={"view": other}, device_id_type=MESH)
    peers = jnp.int32(1)
    for shift, both in ((2, False), (-2, False), (1, True), (-1, True)):
        there = (tile + shift >= 0) & (tile + shift < count)
        peers = peers + jnp.where(there, 2 if both else 1, 0)

        @pl.when(there)
        def _(shift=shift, both=both):
            pl.semaphore_signal(barrier, inc=1, device_id={"tile": tile + shift}, device_id_type=MESH)
            if both:
                pl.semaphore_signal(barrier, inc=1, device_id={"tile": tile + shift, "view": other}, device_id_type=MESH)

    pl.semaphore_wait(barrier, peers)

    def slot(q, n):
        return ext[n].at[pl.ds(core * views, views), pl.ds((BELOW - q) * rows, rows)]

    def mine(n):
        return feat.at[:, :, pl.ds(n * WIDTH, WIDTH)]

    def z_copy(p, n):
        src = mine(n) if p == 0 else slot(2 * p, n)
        return pltpu.make_async_remote_copy(src, slot(2 * p + 2, n), z_send.at[p, n], z_recv.at[p, n], device_id={"tile": tile + 2}, device_id_type=MESH)

    def even_copy(k, n):
        src = mine(n) if k == 0 else slot(2 * k, n)
        return pltpu.make_async_remote_copy(src, slot(2 * k + 1, n), pair_send.at[k, n], pair_recv.at[k, n], device_id={"tile": partner}, device_id_type=MESH)

    def odd_copy(k, n):
        return pltpu.make_async_remote_copy(slot(2 * k + 2, n), slot(2 * k + 1, n), pair_send.at[k, n], pair_recv.at[k, n], device_id={"tile": partner}, device_id_type=MESH)

    def core_copy(q, n):
        src = mine(n) if q == 0 else slot(q, n)
        return pltpu.make_async_remote_copy(src, slot(q, n), core_send.at[q, n], core_recv.at[q, n], device_id={"view": other}, device_id_type=MESH)

    def edge_copy(n, far, side):
        return pltpu.make_async_remote_copy(
            feat.at[:, pl.ds(0, 1), pl.ds(n * WIDTH, WIDTH)],
            ext[n].at[pl.ds(side * views, views), pl.ds(top + rows, 1)],
            edge_send.at[far, n],
            edge_recv.at[far, n],
            device_id={"tile": tile - 1, "view": other if far else core},
            device_id_type=MESH,
        )

    def local_copy(n):
        return pltpu.make_async_copy(mine(n), slot(0, n), local_sem.at[n])

    def out_copy(n):
        return pltpu.make_async_copy(cost.at[n], out.at[n], out_sem.at[n])

    def blank(low, many):
        for n in everything:
            for v in range(2 * views):
                ext[n][v, low : low + many] = jnp.zeros((many, WIDTH, columns), feat.dtype)

    last = tile == count - 1
    upward = tile + 2 < count
    everything = range(parts)

    @pl.when(upward)
    def _():
        for n in everything:
            z_copy(0, n).start()

    @pl.when(odd == 0)
    def _():
        for n in everything:
            even_copy(0, n).start()

    for n in everything:
        local_copy(n).start()
        core_copy(0, n).start()

    @pl.when(tile >= 1)
    def _():
        for n in everything:
            for far in range(2):
                edge_copy(n, far, core).start()

    for q in range(1, BELOW + 1):

        @pl.when(tile < q)
        def _(q=q):
            blank((BELOW - q) * rows, rows)

    @pl.when(last)
    def _():
        blank(top + rows, 1)

    def compute(n):
        for q in range(BELOW + 1):

            @pl.when(tile >= q)
            def _(q=q):
                core_copy(q, n).wait_recv()

        @pl.when(jnp.logical_not(last))
        def _():
            for far in range(2):
                edge_copy(n, far, other if far else core).wait_recv()

        local_copy(n).wait()
        correlate(ext[n], refs, marks, offs, select, moved, cost.at[n], core)
        out_copy(n).start()

    for p in range(3):
        for n in everything:

            @pl.when(tile >= 2 * p + 2)
            def _(p=p, n=n):
                z_copy(p, n).wait_recv()
                if p < 2:

                    @pl.when(upward)
                    def _():
                        z_copy(p + 1, n).start()

                    @pl.when(odd == 0)
                    def _():
                        even_copy(p + 1, n).start()

                @pl.when(odd == 1)
                def _():
                    odd_copy(p, n).start()

                core_copy(2 * p + 2, n).start()

            @pl.when(tile >= 2 * p + 1)
            def _(p=p, n=n):
                even_copy(p, n).wait_recv()
                core_copy(2 * p + 1, n).start()

            if p == 2 and n > 0:
                compute(n - 1)

    compute(parts - 1)

    for n in everything:
        for p in range(3):

            @pl.when(upward & (tile >= 2 * p))
            def _(p=p, n=n):
                z_copy(p, n).wait_send()

            @pl.when((odd == 0) & (tile >= 2 * p))
            def _(p=p, n=n):
                even_copy(p, n).wait_send()

            @pl.when((odd == 1) & (tile >= 2 * p + 2))
            def _(p=p, n=n):
                odd_copy(p, n).wait_send()

        for q in range(BELOW + 1):

            @pl.when(tile >= q)
            def _(q=q, n=n):
                core_copy(q, n).wait_send()

        @pl.when(tile >= 1)
        def _(n=n):
            for far in range(2):
                edge_copy(n, far, core).wait_send()

        out_copy(n).wait()


def correlate(ext, refs, marks, offs, select, moved, cost, half):
    slots = refs.shape[0]
    views, span, width, columns = ext.shape
    planes = ND // 2 + 1
    tall = 10
    own = span - tall
    sums = planes + tall - 1
    first = own - (planes - 1) - 15 * half

    def one(slot, _):
        sources = [(marks[slot, v].astype(jnp.float32).astype(jnp.bfloat16), first - offs[slot, v]) for v in range(views)]
        total = marks[slot, 0]
        for v in range(1, views):
            total = total + marks[slot, v]
        scale = 0.125 / jnp.full((8, columns), total.astype(jnp.float32))
        for m in range(sums):
            rows = [ext[v, start + m] * mark for v, (mark, start) in enumerate(sources)]
            moved[m * width : (m + 1) * width] = (rows[0] + rows[1]) + (rows[2] + rows[3])
        view = refs[slot]
        for low, many in ((0, 4), (4, 4), (8, 2)):
            anchor = ext[view, own + low : own + low + many].reshape(many * width, columns)
            mat = select[: many * 8, : many * width]
            factor = jnp.concatenate([scale] * many, axis=0)
            for k in range(0, planes, 2):
                ks = [k, k + 1] if k + 1 < planes else [k]
                blocks = []
                for kk in ks:
                    at = (low - kk + planes - 1) * width
                    blocks.append(moved[at : at + many * width] * anchor)
                block = jnp.concatenate(blocks, axis=1) if len(blocks) > 1 else blocks[0]
                got = jnp.dot(mat, block, preferred_element_type=jnp.float32)
                for n, kk in enumerate(ks):
                    cost[slot, kk, low * 8 : (low + many) * 8] = (got[:, n * columns : (n + 1) * columns] * factor).astype(jnp.bfloat16)
        return 0

    lax.fori_loop(0, slots, one, 0)


def gathered(features, refs, marks, offs, count):
    views, rows, channels, columns = features.shape
    slots = refs.shape[0]
    n = channels // WIDTH
    planes = ND // 2 + 1
    span = (BELOW + 1) * rows + 1
    select = (jnp.arange(32)[:, None] == jnp.arange(4 * WIDTH)[None, :] // 8).astype(jnp.bfloat16)
    dma = pltpu.SemaphoreType.DMA
    shape = (n, slots, planes, 80, columns)
    smem = pl.BlockSpec(memory_space=pltpu.SMEM)
    return pl.pallas_call(
        functools.partial(gather_kernel, count),
        out_shape=jax.ShapeDtypeStruct(shape, features.dtype),
        in_specs=[pl.BlockSpec(memory_space=pl.ANY), smem, smem, smem, pl.BlockSpec(memory_space=pltpu.VMEM)],
        out_specs=pl.BlockSpec(memory_space=pl.ANY),
        scratch_shapes=[pltpu.VMEM((2 * views, span, WIDTH, columns), features.dtype) for _ in range(n)]
        + [
            pltpu.VMEM(((planes + 9) * WIDTH, columns), features.dtype),
            pltpu.VMEM(shape, features.dtype),
            dma((n,)),
            dma((n,)),
            dma((3, n)),
            dma((3, n)),
            dma((3, n)),
            dma((3, n)),
            dma((BELOW + 1, n)),
            dma((BELOW + 1, n)),
            dma((2, n)),
            dma((2, n)),
        ],
        compiler_params=pltpu.CompilerParams(collective_id=0, has_side_effects=True, vmem_limit_bytes=60 * 1024 * 1024),
    )(features, refs, marks, offs, select)


def volume_kernel(cost, weight, bias, out, taps, ring):
    half = lax.axis_index("view")
    parts, planes, columns = cost.shape[0], cost.shape[2], cost.shape[4]
    tall = 10
    groups = parts * 8
    lane = lax.broadcasted_iota(jnp.int32, (groups, columns), 1)
    spare = jnp.zeros((128 - 3 * groups, columns), jnp.float32)
    taps[planes * half] = jnp.zeros_like(taps[0])

    def spread(k):
        for pair in range(0, tall, 2):
            both = [cost[n, 0, k, pair * 8 : pair * 8 + 16].astype(jnp.float32) for n in range(parts)]
            for row in range(2):
                here = jnp.concatenate([one[row * 8 : row * 8 + 8] for one in both], axis=0)
                left = jnp.where(lane == 0, 0.0, pltpu.roll(here, 1, 1))
                right = jnp.where(lane == columns - 1, 0.0, pltpu.roll(here, columns - 1, 1))
                block = jnp.concatenate([left, here, right, spare], axis=0)
                taps[k + 1 - half, (pair + row) * 128 : (pair + row + 1) * 128] = block.astype(jnp.bfloat16)

    for k in range(planes):
        spread(k)

    def convolve(plane):
        for row in range(0, 8, 4):
            block = jnp.concatenate([taps[plane, (row + n) * 128 : (row + n + 4) * 128] for n in (0, 2)], axis=1)
            got = jnp.dot(weight[...], block, preferred_element_type=jnp.float32)
            for n in range(4):
                low = (n % 2) * 96
                piece = got[low : low + 96, (n // 2) * columns : (n // 2 + 1) * columns]
                ring[2, row + n] = ring[1, row + n] + piece[64:]
                ring[1, row + n] = ring[0, row + n] + piece[32:64]
                ring[0, row + n] = piece[:32]

    def finish(plane):
        done = jnp.maximum(ring[2] + bias[...][None], 0.0)
        out[0, :, plane - 2] = jnp.swapaxes(done, 0, 1).astype(jnp.bfloat16)

    for plane in range(planes + 1):
        convolve(plane)
        if plane >= 2:
            finish(plane)


def volume(cost, conv_weight, conv_bias):
    parts, slots, planes, tall, columns = cost.shape
    made, groups = conv_weight.shape[3], conv_weight.shape[4]
    weight = jnp.transpose(conv_weight, (0, 3, 1, 2, 4)).reshape(3 * made, 3, 3 * groups)
    weight = jnp.pad(weight, ((0, 0), (0, 0), (0, 128 - 3 * groups))).reshape(3 * made, 384)
    weight = jnp.concatenate([jnp.pad(weight, ((0, 0), (128 * n, 128 - 128 * n))) for n in range(2)], axis=0)
    bias = jnp.broadcast_to(conv_bias[:, None], (made, columns))
    shape = (slots, made, ND // 2, 8, columns)
    return pl.pallas_call(
        volume_kernel,
        grid=(slots,),
        out_shape=jax.ShapeDtypeStruct(shape, jnp.bfloat16),
        in_specs=[
            pl.BlockSpec((parts, 1, planes, tall, columns), lambda r: (0, r, 0, 0, 0)),
            pl.BlockSpec(weight.shape, lambda r: (0, 0)),
            pl.BlockSpec(bias.shape, lambda r: (0, 0)),
        ],
        out_specs=pl.BlockSpec((1,) + shape[1:], lambda r: (r, 0, 0, 0, 0)),
        scratch_shapes=[
            pltpu.VMEM((planes + 1, 10 * 128, columns), jnp.bfloat16),
            pltpu.VMEM((3, 8, made, columns), jnp.float32),
        ],
        compiler_params=pltpu.CompilerParams(vmem_limit_bytes=60 * 1024 * 1024),
    )(cost, weight, bias)


def shards(count, features, ref_views, intersection, offsets, conv_weight, conv_bias):
    cost = gathered(features, ref_views, intersection, offsets, count)
    return volume(cost, conv_weight, conv_bias)


def solution(mesh):
    placed = (
        P(("groups", "view"), "tile", None, None),
        P("groups"),
        P("groups", None),
        P("groups", None),
        P(),
        P(),
    )
    return jax.shard_map(
        functools.partial(shards, mesh.shape["tile"]),
        mesh=mesh,
        in_specs=placed,
        out_specs=P("groups", None, "view", "tile", None),
        check_vma=False,
    )
```

```python
import functools

import jax
import jax.numpy as jnp
from jax import lax
from jax.experimental import pallas as pl
from jax.experimental.pallas import tpu as pltpu
from jax.sharding import PartitionSpec as P

ND = 32
OFF = 17
BELOW = 6
MESH = pl.DeviceIdType.MESH
WIDTH = 64


def gather_kernel(count, feat, refs, marks, offs, out, *scratch):
    views, rows, channels, columns = feat.shape
    parts = channels // WIDTH
    ext, rest = scratch[:parts], scratch[parts:]
    select, moved, cost, local_sem, out_sem, z_send, z_recv, pair_send, pair_recv, core_send, core_recv, edge_send, edge_recv = rest
    tile = lax.axis_index("tile")
    core = lax.axis_index("view")
    other = 1 - core
    odd = tile % 2
    partner = tile + 1 - 2 * odd
    top = BELOW * rows

    barrier = pltpu.get_barrier_semaphore()
    pl.semaphore_signal(barrier, inc=1, device_id={"view": other}, device_id_type=MESH)
    peers = jnp.int32(1)
    for shift, both in ((2, False), (-2, False), (1, True), (-1, True)):
        there = (tile + shift >= 0) & (tile + shift < count)
        peers = peers + jnp.where(there, 2 if both else 1, 0)

        @pl.when(there)
        def _(shift=shift, both=both):
            pl.semaphore_signal(barrier, inc=1, device_id={"tile": tile + shift}, device_id_type=MESH)
            if both:
                pl.semaphore_signal(barrier, inc=1, device_id={"tile": tile + shift, "view": other}, device_id_type=MESH)

    pl.semaphore_wait(barrier, peers)

    def slot(q, n):
        return ext[n].at[pl.ds(core * views, views), pl.ds((BELOW - q) * rows, rows)]

    def mine(n):
        return feat.at[:, :, pl.ds(n * WIDTH, WIDTH)]

    def z_copy(p, n):
        src = mine(n) if p == 0 else slot(2 * p, n)
        return pltpu.make_async_remote_copy(src, slot(2 * p + 2, n), z_send.at[p, n], z_recv.at[p, n], device_id={"tile": tile + 2}, device_id_type=MESH)

    def even_copy(k, n):
        src = mine(n) if k == 0 else slot(2 * k, n)
        return pltpu.make_async_remote_copy(src, slot(2 * k + 1, n), pair_send.at[k, n], pair_recv.at[k, n], device_id={"tile": partner}, device_id_type=MESH)

    def odd_copy(k, n):
        return pltpu.make_async_remote_copy(slot(2 * k + 2, n), slot(2 * k + 1, n), pair_send.at[k, n], pair_recv.at[k, n], device_id={"tile": partner}, device_id_type=MESH)

    def core_copy(q, n):
        src = mine(n) if q == 0 else slot(q, n)
        return pltpu.make_async_remote_copy(src, slot(q, n), core_send.at[q, n], core_recv.at[q, n], device_id={"view": other}, device_id_type=MESH)

    def edge_copy(n, far, side):
        return pltpu.make_async_remote_copy(
            feat.at[:, pl.ds(0, 1), pl.ds(n * WIDTH, WIDTH)],
            ext[n].at[pl.ds(side * views, views), pl.ds(top + rows, 1)],
            edge_send.at[far, n],
            edge_recv.at[far, n],
            device_id={"tile": tile - 1, "view": other if far else core},
            device_id_type=MESH,
        )

    def local_copy(n):
        return pltpu.make_async_copy(mine(n), slot(0, n), local_sem.at[n])

    def out_copy(n):
        return pltpu.make_async_copy(cost.at[n], out.at[n], out_sem.at[n])

    def blank(low, many):
        for n in everything:
            for v in range(2 * views):
                ext[n][v, low : low + many] = jnp.zeros((many, WIDTH, columns), feat.dtype)

    last = tile == count - 1
    upward = tile + 2 < count
    everything = range(parts)

    @pl.when(upward)
    def _():
        for n in everything:
            z_copy(0, n).start()

    @pl.when(odd == 0)
    def _():
        for n in everything:
            even_copy(0, n).start()

    for n in everything:
        local_copy(n).start()
        core_copy(0, n).start()

    @pl.when(tile >= 1)
    def _():
        for n in everything:
            for far in range(2):
                edge_copy(n, far, core).start()

    group = lax.broadcasted_iota(jnp.int32, select.shape, 0)
    channel = lax.broadcasted_iota(jnp.int32, select.shape, 1)
    member = (channel >= group * 8) & (channel < group * 8 + 8)
    select[...] = jnp.where(member, 1.0, 0.0).astype(select.dtype)

    for q in range(1, BELOW + 1):

        @pl.when(tile < q)
        def _(q=q):
            blank((BELOW - q) * rows, rows)

    @pl.when(last)
    def _():
        blank(top + rows, 1)

    def compute(n):
        for q in range(BELOW + 1):

            @pl.when(tile >= q)
            def _(q=q):
                core_copy(q, n).wait_recv()

        @pl.when(jnp.logical_not(last))
        def _():
            for far in range(2):
                edge_copy(n, far, other if far else core).wait_recv()

        local_copy(n).wait()
        correlate(ext[n], refs, marks, offs, select, moved, cost.at[n], core)
        out_copy(n).start()

    def paired(p, n):
        @pl.when(tile >= 2 * p + 1)
        def _():
            even_copy(p, n).wait_recv()
            core_copy(2 * p + 1, n).start()

    for p in range(3):
        for n in everything:

            @pl.when(tile >= 2 * p + 2)
            def _(p=p, n=n):
                z_copy(p, n).wait_recv()
                if p < 2:

                    @pl.when(upward)
                    def _():
                        z_copy(p + 1, n).start()

                    @pl.when(odd == 0)
                    def _():
                        even_copy(p + 1, n).start()

                @pl.when(odd == 1)
                def _():
                    odd_copy(p, n).start()

                core_copy(2 * p + 2, n).start()

            if p + n > 0:
                paired(*((p, n - 1) if n > 0 else (p - 1, parts - 1)))

            if p == 2 and n > 0:
                compute(n - 1)

    paired(2, parts - 1)
    compute(parts - 1)

    for n in everything:
        for p in range(3):

            @pl.when(upward & (tile >= 2 * p))
            def _(p=p, n=n):
                z_copy(p, n).wait_send()

            @pl.when((odd == 0) & (tile >= 2 * p))
            def _(p=p, n=n):
                even_copy(p, n).wait_send()

            @pl.when((odd == 1) & (tile >= 2 * p + 2))
            def _(p=p, n=n):
                odd_copy(p, n).wait_send()

        for q in range(BELOW + 1):

            @pl.when(tile >= q)
            def _(q=q, n=n):
                core_copy(q, n).wait_send()

        @pl.when(tile >= 1)
        def _(n=n):
            for far in range(2):
                edge_copy(n, far, core).wait_send()

        out_copy(n).wait()


def correlate(ext, refs, marks, offs, select, moved, cost, half):
    slots = refs.shape[0]
    views, span, width, columns = ext.shape
    planes = ND // 2 + 1
    tall = 10
    own = span - tall
    sums = planes + tall - 1
    first = own - (planes - 1) - 15 * half

    def one(slot, _):
        sources = [(marks[slot, v].astype(jnp.float32).astype(jnp.bfloat16), first - offs[slot, v]) for v in range(views)]
        total = marks[slot, 0]
        for v in range(1, views):
            total = total + marks[slot, v]
        scale = 0.125 / jnp.full((8, columns), total.astype(jnp.float32))
        for m in range(sums):
            rows = [ext[v, start + m] * mark for v, (mark, start) in enumerate(sources)]
            moved[m * width : (m + 1) * width] = (rows[0] + rows[1]) + (rows[2] + rows[3])
        view = refs[slot]
        for low, many in ((0, 4), (4, 4), (8, 2)):
            anchor = ext[view, own + low : own + low + many].reshape(many * width, columns)
            mat = select[: many * 8, : many * width]
            factor = jnp.concatenate([scale] * many, axis=0)
            for k in range(0, planes, 2):
                ks = [k, k + 1] if k + 1 < planes else [k]
                blocks = []
                for kk in ks:
                    at = (low - kk + planes - 1) * width
                    blocks.append(moved[at : at + many * width] * anchor)
                block = jnp.concatenate(blocks, axis=1) if len(blocks) > 1 else blocks[0]
                got = jnp.dot(mat, block, preferred_element_type=jnp.float32)
                for n, kk in enumerate(ks):
                    cost[slot, kk, low * 8 : (low + many) * 8] = (got[:, n * columns : (n + 1) * columns] * factor).astype(jnp.bfloat16)
        return 0

    lax.fori_loop(0, slots, one, 0)


def gathered(features, refs, marks, offs, count):
    views, rows, channels, columns = features.shape
    slots = refs.shape[0]
    n = channels // WIDTH
    planes = ND // 2 + 1
    span = (BELOW + 1) * rows + 1
    dma = pltpu.SemaphoreType.DMA
    shape = (n, slots, planes, 80, columns)
    smem = pl.BlockSpec(memory_space=pltpu.SMEM)
    return pl.pallas_call(
        functools.partial(gather_kernel, count),
        out_shape=jax.ShapeDtypeStruct(shape, features.dtype),
        in_specs=[pl.BlockSpec(memory_space=pl.ANY), smem, smem, smem],
        out_specs=pl.BlockSpec(memory_space=pl.ANY),
        scratch_shapes=[pltpu.VMEM((2 * views, span, WIDTH, columns), features.dtype) for _ in range(n)]
        + [
            pltpu.VMEM((32, 4 * WIDTH), features.dtype),
            pltpu.VMEM(((planes + 9) * WIDTH, columns), features.dtype),
            pltpu.VMEM(shape, features.dtype),
            dma((n,)),
            dma((n,)),
            dma((3, n)),
            dma((3, n)),
            dma((3, n)),
            dma((3, n)),
            dma((BELOW + 1, n)),
            dma((BELOW + 1, n)),
            dma((2, n)),
            dma((2, n)),
        ],
        compiler_params=pltpu.CompilerParams(collective_id=0, has_side_effects=True, vmem_limit_bytes=60 * 1024 * 1024),
    )(features, refs, marks, offs)


def volume_kernel(cost, weight, shift, out, taps, ring, bias):
    for o in range(bias.shape[0]):
        bias[o : o + 1] = jnp.full((1, bias.shape[1]), shift[o])
    half = lax.axis_index("view")
    parts, planes, columns = cost.shape[0], cost.shape[2], cost.shape[4]
    tall = 10
    groups = parts * 8
    lane = lax.broadcasted_iota(jnp.int32, (groups, columns), 1)
    spare = jnp.zeros((128 - 3 * groups, columns), jnp.float32)
    taps[planes * half] = jnp.zeros_like(taps[0])

    def spread(k):
        for pair in range(0, tall, 2):
            both = [cost[n, 0, k, pair * 8 : pair * 8 + 16].astype(jnp.float32) for n in range(parts)]
            for row in range(2):
                here = jnp.concatenate([one[row * 8 : row * 8 + 8] for one in both], axis=0)
                left = jnp.where(lane == 0, 0.0, pltpu.roll(here, 1, 1))
                right = jnp.where(lane == columns - 1, 0.0, pltpu.roll(here, columns - 1, 1))
                block = jnp.concatenate([left, here, right, spare], axis=0)
                taps[k + 1 - half, (pair + row) * 128 : (pair + row + 1) * 128] = block.astype(jnp.bfloat16)

    for k in range(planes):
        spread(k)

    def convolve(plane):
        for row in range(0, 8, 4):
            block = jnp.concatenate([taps[plane, (row + n) * 128 : (row + n + 4) * 128] for n in (0, 2)], axis=1)
            got = jnp.dot(weight[...], block, preferred_element_type=jnp.float32)
            for n in range(4):
                low = (n % 2) * 96
                piece = got[low : low + 96, (n // 2) * columns : (n // 2 + 1) * columns]
                ring[2, row + n] = ring[1, row + n] + piece[64:]
                ring[1, row + n] = ring[0, row + n] + piece[32:64]
                ring[0, row + n] = piece[:32]

    def finish(plane):
        done = jnp.maximum(ring[2] + bias[...][None], 0.0)
        out[0, :, plane - 2] = jnp.swapaxes(done, 0, 1).astype(jnp.bfloat16)

    for plane in range(planes + 1):
        convolve(plane)
        if plane >= 2:
            finish(plane)


def volume(cost, conv_weight, conv_bias):
    parts, slots, planes, tall, columns = cost.shape
    made, groups = conv_weight.shape[3], conv_weight.shape[4]
    weight = jnp.transpose(conv_weight, (0, 3, 1, 2, 4)).reshape(3 * made, 3, 3 * groups)
    weight = jnp.pad(weight, ((0, 0), (0, 0), (0, 128 - 3 * groups))).reshape(3 * made, 384)
    weight = jnp.concatenate([jnp.pad(weight, ((0, 0), (128 * n, 128 - 128 * n))) for n in range(2)], axis=0)
    shape = (slots, made, ND // 2, 8, columns)
    return pl.pallas_call(
        volume_kernel,
        grid=(slots,),
        out_shape=jax.ShapeDtypeStruct(shape, jnp.bfloat16),
        in_specs=[
            pl.BlockSpec((parts, 1, planes, tall, columns), lambda r: (0, r, 0, 0, 0)),
            pl.BlockSpec(weight.shape, lambda r: (0, 0)),
            pl.BlockSpec(memory_space=pltpu.SMEM),
        ],
        out_specs=pl.BlockSpec((1,) + shape[1:], lambda r: (r, 0, 0, 0, 0)),
        scratch_shapes=[
            pltpu.VMEM((planes + 1, 10 * 128, columns), jnp.bfloat16),
            pltpu.VMEM((3, 8, made, columns), jnp.float32),
            pltpu.VMEM((made, columns), jnp.float32),
        ],
        compiler_params=pltpu.CompilerParams(vmem_limit_bytes=60 * 1024 * 1024),
    )(cost, weight, conv_bias)


def shards(count, features, ref_views, intersection, offsets, conv_weight, conv_bias):
    cost = gathered(features, ref_views, intersection, offsets, count)
    return volume(cost, conv_weight, conv_bias)


def solution(mesh):
    placed = (
        P(("groups", "view"), "tile", None, None),
        P("groups"),
        P("groups", None),
        P("groups", None),
        P(),
        P(),
    )
    return jax.shard_map(
        functools.partial(shards, mesh.shape["tile"]),
        mesh=mesh,
        in_specs=placed,
        out_specs=P("groups", None, "view", "tile", None),
        check_vma=False,
    )
```
